128 devices in a mesh: row: 8 (over y, core), col: 16 (over x, z).
Axes of the slice: x: 4, y: 4, z: 4, core: 2. Of those that a mesh axis runs over, the one named last changes fastest.
Arguments:
- blk_u: bfloat16 [96, 128, 64, 512], P('row', 'col'), may hold values from -6 to 6
- blk_v: bfloat16 [96, 128, 64, 512], P('row', 'col'), may hold values from -0.75 to 0.75
- prow_u: bfloat16 [96, 64, 512], P('col'), may hold values from -6 to 6
- prow_v: bfloat16 [96, 64, 512], P('col'), may hold values from -0.1875 to 0.1875
- pcol_u: bfloat16 [128, 64, 512], P('row'), may hold values from -6 to 6
- pcol_v: bfloat16 [128, 64, 512], P('row'), may hold values from -0.1875 to 0.1875
- linv: bfloat16 [512, 512], P('col'), may hold values from -0.15 to 1.4, as said below
- omega: bfloat16 [64, 512], replicated, may hold values from -0.25 to 0.25
- child_u: bfloat16 [2048, 64, 512], P(('row', 'col')), may hold values from -6 to 6
- child_v: bfloat16 [2048, 64, 512], P(('row', 'col')), may hold values from -0.75 to 0.75
- child_dest: int32 [2048, 1], P(('row', 'col')), may hold values from 0 to 15; in each aligned block of 16 rows (0 to 15, 16 to 31, ...) at most 2 rows name the same one
- child_block: int32 [2048], P(('row', 'col')), may hold values from 0 to 95
Outputs:
- sketch: bfloat16 [96, 128, 64, 512], P('row', 'col')
- prow_l: bfloat16 [96, 64, 512], P('col')
- pcol_l: bfloat16 [128, 64, 512], P('row')
The draws below stay inside these ranges and needn't reach their ends.
Inputs may be any that keep to these rules, and one draw needn't show every extreme that they name: `linv`: lower triangular with diagonal entries of about 0.6 to 1.4. `child_dest`: in the 16 child blocks of one device at most 2 name the same column index, and some column index is named 2 times.
All inputs are finite; a program needn't handle non-finite values.
Results may differ from the reference program's by a relative error of at most 0.0065.
Values may be sent and summed in bfloat16 or wider, within the bound.
A program may use at most 192 MiB of HBM per device.

```python
import math
import jax
import jax.numpy as jnp
import numpy as np
from jax import lax

B = 512
R = 64
ROWB = 12
COLB = 8
CB = 16
CAP = 2
NA = 96
NB = 128
CHILD = 2048
N_COL = 16


def draw_linv(key, part):
    key = jax.random.fold_in(key, 11)
    first, second = jax.random.split(key)
    spread = jax.random.normal(first, (B, B), jnp.float32) * (0.6 / B ** 0.5)
    spread = jnp.clip(spread, -0.1494, 0.1494)
    lower = jnp.tril(spread, -1)
    diag_vals = jax.random.uniform(second, (B,), jnp.float32, 0.6, 1.4)
    return (lower + jnp.diag(diag_vals)).astype(jnp.bfloat16)


def with_ends(array, rng, low, high):
    place = [jax.random.randint(jax.random.fold_in(rng, axis), (), 0, length) for axis, length in enumerate(array.shape)]
    main_axis = array.shape.index(max(array.shape))
    next_to = place[:main_axis] + [(place[main_axis] + 1) % array.shape[main_axis]] + place[main_axis + 1:]
    return array.at[tuple(place)].set(low).at[tuple(next_to)].set(high)


def level_of(key, shape, cuts, smallest, top_value):
    def one(dim, blocks):
        steps = jax.random.uniform(jax.random.fold_in(jax.random.fold_in(key, 6), dim), (blocks,), jnp.float32, smallest / len(cuts), top_value / len(cuts))
        return jnp.repeat(jnp.exp(steps), shape[dim] // blocks).reshape((-1,) + (1,) * (len(shape) - dim - 1))

    level = one(*cuts[0])
    for cut in cuts[1:]:
        level = level * one(*cut)
    return level


def shared_out(key, own, number, rows, amount, top, limit, lean):
    order = jax.random.permutation(key, amount)
    heavy_load, usual = load_shares(amount, rows * top, limit, lean, True), load_shares(amount, rows * top, limit, lean, False)
    places = jnp.arange(amount)

    def named(lengths, rotation):
        used = int((lengths > 0).sum())
        fixed = max(1, used // 4)
        moved = fixed + (places - fixed + rotation * (used - fixed)) % max(1, amount - fixed)
        return jnp.zeros((amount,), jnp.int32).at[order[jnp.where(places < fixed, places, moved)]].set(jnp.asarray(lengths, jnp.int32))

    lengths = jnp.where(number % 4 == 0, named(heavy_load, number // 4), named(usual, number - number // 4 - 1))
    mixed = jax.random.permutation(jax.random.fold_in(own, 3), amount)
    donor, receiver = mixed[0:amount // 2 * 2:2], mixed[1:amount // 2 * 2:2]
    slack = jnp.minimum(lengths[donor] - 1, limit - lengths[receiver]) // 2
    slack = jnp.where((donor == order[0]) | (receiver == order[0]) | (lengths[receiver] == 0), 0, jnp.maximum(slack, 0))
    moved = jax.random.randint(jax.random.fold_in(own, 4), (amount // 2,), 0, 1 << 20) % (slack + 1)
    lengths = lengths.at[donor].add(-moved).at[receiver].add(moved)
    members = jnp.searchsorted(jnp.cumsum(lengths), jnp.arange(rows * top), side="right").astype(jnp.int32)
    listing = members.reshape(top, rows).T
    listing = listing[jax.random.permutation(jax.random.fold_in(own, 1), rows)]
    rotation = jax.random.randint(jax.random.fold_in(own, 2), (rows, 1), 0, top)
    return jnp.take_along_axis(listing, (jnp.arange(top)[None, :] + rotation) % top, axis=1)


def load_shares(count, total, limit, lean, full):
    weights = [(1 << 20) // math.isqrt(rank ** lean) + 1 for rank in range(1, count + 1)]
    largest = limit if full else min(limit, max(-(-total // count), total * weights[0] // sum(weights)))
    least = 1 if total - largest >= count - 1 else 0
    holding, surplus = [largest] + [least] * (count - 1), total - largest - least * (count - 1)
    while surplus > 0:
        movable = [i for i in range(1, count) if holding[i] < largest] or [i for i in range(1, count) if holding[i] < limit]
        whole, budget = sum([weights[i] for i in movable]), surplus
        for i in movable:
            extra = min(limit - holding[i], max(1, budget * weights[i] // whole), surplus)
            holding[i] = holding[i] + extra
            surplus = surplus - extra
    return np.array(holding)


def centred(stream_key, shape, deviation, limit, pieces=(), kind=jnp.bfloat16):
    values = deviation * jax.random.normal(stream_key, shape, jnp.float32)
    if pieces:
        values = values * level_of(stream_key, shape, pieces, -0.22, 0.18)
    return jnp.clip(values, -limit, limit).astype(kind)


def setup_inputs(seed: int = 0) -> dict:
    key_of = jax.random.split(jax.random.key(seed), 13)
    blk_u = centred(key_of[0], (NA, NB, R, B), 1.0, 6.0, ((0, 8), (1, 16)))
    blk_v = centred(key_of[1], (NA, NB, R, B), R ** -0.5, 0.75, ((0, 8), (1, 16)))
    prow_u = centred(key_of[2], (NA, R, B), 1.0, 6.0, ((0, 16),))
    prow_v = centred(key_of[3], (NA, R, B), (R * 16) ** -0.5, 0.1875, ((0, 16),))
    pcol_u = centred(key_of[4], (NB, R, B), 1.0, 6.0, ((0, 8),))
    pcol_v = centred(key_of[5], (NB, R, B), (R * 16) ** -0.5, 0.1875, ((0, 8),))
    linv = draw_linv(jax.random.fold_in(key_of[12], 71), 0)
    omega = centred(key_of[7], (R, B), B ** -0.5, 0.25)
    child_u = centred(key_of[8], (CHILD, R, B), 1.0, 6.0, ((0, 128),))
    child_v = centred(key_of[9], (CHILD, R, B), R ** -0.5, 0.75, ((0, 128),))
    child_dest_keys = jax.random.split(jax.random.fold_in(key_of[10], 1), CHILD // CB)
    child_dest_turns = jax.random.permutation(jax.random.fold_in(key_of[10], 3), CHILD // CB)
    child_dest = jax.vmap(lambda own, number: shared_out(jax.random.fold_in(key_of[10], 2), own, number, CB, N_COL, 1, CAP, 2))(child_dest_keys, child_dest_turns).reshape((CHILD, 1))
    child_block = with_ends(jax.random.randint(key_of[11], (CHILD,), 0, ROWB * COLB), jax.random.fold_in(key_of[11], 1), 0, (ROWB * COLB) - 1).astype(jnp.int32)
    return dict(blk_u=blk_u, blk_v=blk_v, prow_u=prow_u, prow_v=prow_v, pcol_u=pcol_u, pcol_v=pcol_v, linv=linv, omega=omega, child_u=child_u, child_v=child_v, child_dest=child_dest, child_block=child_block)


def reference(blk_u, blk_v, prow_u, prow_v, pcol_u, pcol_v, linv, omega, child_u, child_v, child_dest, child_block):
    fl = jnp.float32
    inverse = linv.astype(fl)
    test = omega.astype(fl)
    prow_l = jnp.einsum('nrb,kb->nrk', prow_v.astype(fl), inverse).astype(jnp.bfloat16)
    pcol_l = jnp.einsum('nrb,kb->nrk', pcol_v.astype(fl), inverse).astype(jnp.bfloat16)
    col_sketch = jnp.einsum('jqb,sb->jqs', pcol_u.astype(fl), test).astype(jnp.bfloat16)
    far_l = pcol_l.astype(fl)
    far_q = col_sketch.astype(fl)

    def one_row(items):
        left, right, near_u, near_l = items
        proj = jnp.einsum('jrb,qb->jrq', right.astype(fl), test).astype(jnp.bfloat16)
        base = jnp.einsum('jrq,jrb->jqb', proj.astype(fl), left.astype(fl))
        inner = jnp.einsum('rb,jqb->jrq', near_l.astype(fl), far_l)
        coupled = jnp.einsum('jrq,jqs->jrs', inner, far_q, precision=lax.Precision.HIGHEST).astype(jnp.bfloat16)
        update = jnp.einsum('jrs,rb->jsb', coupled.astype(fl), near_u.astype(fl))
        return base - update

    result = lax.map(one_row, (blk_u, blk_v, prow_u, prow_l))
    weight = jnp.einsum('crb,qb->crq', child_v.astype(fl), test).astype(jnp.bfloat16)
    contrib = jnp.einsum('crq,crb->cqb', weight.astype(fl), child_u.astype(fl))
    owner_row = (jnp.arange(CHILD, dtype=jnp.int32) // CB) // N_COL
    target_row = (owner_row * ROWB + child_block // COLB).astype(jnp.int32)
    target_col = (child_dest[:, 0] * COLB + child_block % COLB).astype(jnp.int32)
    result = result.at[target_row, target_col].add(contrib)
    return result.astype(jnp.bfloat16), prow_l, pcol_l
```

```python
import functools

import jax
import jax.numpy as jnp
from jax import lax
from jax.experimental import pallas as pl
from jax.experimental.pallas import tpu as pltpu
from jax.sharding import PartitionSpec as P

MESH = pl.DeviceIdType.MESH
HALF = jnp.bfloat16
FULL = jnp.float32
SIDE = 4
ROWS, COLS = 2 * SIDE, SIDE * SIDE
OFFSETS = sorted(
    [(dx, dz) for dx in range(SIDE) for dz in range(SIDE)],
    key=lambda o: (o == (0, 0), min(o[0], SIDE - o[0]) + min(o[1], SIDE - o[1])),
)


def nt(a, b):
    return lax.dot_general(a, b, (((1,), (1,)), ((), ())), preferred_element_type=FULL)


def nn(a, b):
    return lax.dot_general(a, b, (((1,), (0,)), ((), ())), preferred_element_type=FULL)


def block_diagonal(a, rank):
    n = a.shape[1] // rank
    tall = jnp.concatenate([a] * n, 0)
    row = lax.broadcasted_iota(jnp.int32, tall.shape, 0) // rank
    col = lax.broadcasted_iota(jnp.int32, tall.shape, 1) // rank
    return jnp.where(row == col, tall, jnp.zeros_like(tall))


def sketch_of(om, v, u, rank):
    proj = nt(om, v).astype(HALF)
    return nn(block_diagonal(proj, rank), u)


def exchange_kernel(
    blk_u, blk_v, prow_u, prow_v, pcol_u, pcol_v, linv, omega, child_u, child_v, cdest, cblock,
    t_out, rcv, lab, prow_l, pcol_l,
    cu, cv, om, snd, lsnd, lin, pu, pv, bu, bv, pcu, pcv, pcl, pvo, prl, gt,
    local, chs, chr_, las, lar, lis, lir, sib, prs, prr, gs, gr, bsem, tsem,
):
    row, col = lax.axis_index("row"), lax.axis_index("col")
    x, z = col // SIDE, col % SIDE
    y, core = row // 2, row % 2
    rank, order = om.shape
    held = prow_v.shape[0]
    half_rows = linv.shape[0] // 2
    count = child_u.shape[0]
    rows, cols = blk_u.shape[0], blk_u.shape[1]

    def dev(x, y, z, core):
        return (2 * (y % SIDE) + core % 2, SIDE * (x % SIDE) + z % SIDE)

    sibling = dev(x, y, z, 1 - core)

    def remote(src, dst, send, recv, to):
        return pltpu.make_async_remote_copy(
            src_ref=src, dst_ref=dst, send_sem=send, recv_sem=recv, device_id=to,
            device_id_type=MESH,
        )

    first = [
        pltpu.make_async_copy(child_v, cv, local.at[0]),
        pltpu.make_async_copy(child_u, cu, local.at[1]),
        pltpu.make_async_copy(omega, om, local.at[2]),
        pltpu.make_async_copy(
            linv.at[pl.ds(half_rows * core, half_rows)], lin.at[col, core], local.at[3]
        ),
    ]
    for copy in first:
        copy.start()

    to_z = (z + y - x + SIDE) % SIDE
    targets = [(x + core + 2 * i) % SIDE for i in range(2)]
    to_self = [
        (t == x) & (x == y) & (to_z == z) & (z // 2 == core) for t in targets
    ]
    sources = []
    for e in range(2):
        sz = 2 * core + e
        sources.append((y, (y + z - sz + SIDE) % SIDE, sz, (x - y + SIDE) % 2))
    from_self = [
        (s[0] == x) & (s[1] == y) & (s[2] == z) & (s[3] == core) for s in sources
    ]

    barrier = pltpu.get_barrier_semaphore()

    def greet(to):
        pl.semaphore_signal(barrier, 1, device_id=to, device_id_type=MESH)

    for dx, dz in OFFSETS[:-1]:
        greet(dev(x + dx, y, z + dz, core))
    for dy in range(SIDE):
        for dc in range(2):
            if dy or dc:
                greet(dev(x, y + dy, z, core + dc))
    awaited = COLS - 1 + ROWS - 1
    for i in range(2):
        @pl.when(jnp.logical_not(to_self[i]))
        def _():
            greet(dev(targets[i], x, to_z, z // 2))

        @pl.when(jnp.logical_not(from_self[i]))
        def _():
            greet(dev(*sources[i]))

        awaited += 2 - to_self[i].astype(jnp.int32) - from_self[i].astype(jnp.int32)
    pl.semaphore_wait(barrier, awaited)

    lin_copies = []
    for o, (dx, dz) in enumerate(OFFSETS[:-1]):
        copy = remote(
            linv.at[pl.ds(half_rows * core, half_rows)], lin.at[col, core],
            lis.at[o], lir.at[o], dev(x + dx, y, z + dz, core),
        )
        copy.start()
        lin_copies.append(copy)

    place = held * (z % 2)

    def panel_copy(i, a, which):
        src, dst = ((prow_u, pu), (prow_v, pv))[which]
        return remote(
            src, dst.at[pl.ds(place, held)], prs.at[2 * i + which], prr.at[2 * (z % 2) + which], a
        )

    for i in range(2):
        for which in range(2):
            @pl.when(jnp.logical_not(to_self[i]))
            def _():
                panel_copy(i, dev(targets[i], x, to_z, z // 2), which).start()

            @pl.when(to_self[i])
            def _():
                src, dst = ((prow_u, pu), (prow_v, pv))[which]
                pltpu.make_async_copy(
                    src, dst.at[pl.ds(place, held)], prs.at[2 * i + which]
                ).start()

    for copy in first[:3]:
        copy.wait()
    lane = lax.broadcasted_iota(jnp.int32, lsnd.shape[1:], 1)
    child_copies = []
    for o, (dx, dz) in enumerate(OFFSETS):
        dest = SIDE * ((x + dx) % SIDE) + (z + dz) % SIDE

        def find(c, found, dest=dest):
            one, two = found
            hit = cdest[c, 0] == dest
            two = jnp.where(hit & (one >= 0), c, two)
            one = jnp.where(hit & (one < 0), c, one)
            return one, two

        one, two = lax.fori_loop(0, count, find, (jnp.int32(-1), jnp.int32(-1)))
        label_one = jnp.where(one >= 0, cblock[jnp.maximum(one, 0)], -1)
        label_two = jnp.where(two >= 0, cblock[jnp.maximum(two, 0)], -1)
        one, two = jnp.maximum(one, 0), jnp.maximum(two, 0)
        lsnd[o] = jnp.where(lane == 0, label_one, label_two)
        v = jnp.concatenate([cv[one], cv[two]], 0)
        u = jnp.concatenate([cu[one], cu[two]], 0)
        snd[o] = sketch_of(om[...], v, u, rank).astype(HALF)
        if (dx, dz) == (0, 0):
            copies = [
                pltpu.make_async_copy(snd.at[o], rcv.at[col], chs.at[o]),
                pltpu.make_async_copy(lsnd.at[o], lab.at[col], las.at[o]),
            ]
        else:
            to = dev(x + dx, y, z + dz, core)
            copies = [
                remote(snd.at[o], rcv.at[col], chs.at[o], chr_.at[o], to),
                remote(lsnd.at[o], lab.at[col], las.at[o], lar.at[o], to),
            ]
        for copy in copies:
            copy.start()
        child_copies += copies

    second = [
        pltpu.make_async_copy(pcol_v, pcv, local.at[4]),
        pltpu.make_async_copy(prow_v, pvo, local.at[5]),
        pltpu.make_async_copy(pcol_u, pcu, local.at[6]),
    ]
    for copy in second:
        copy.start()

    def block_copies(i):
        return (
            pltpu.make_async_copy(blk_u.at[i], bu.at[i], bsem.at[0, i]),
            pltpu.make_async_copy(blk_v.at[i], bv.at[i], bsem.at[1, i]),
        )

    for i in range(rows):
        for copy in block_copies(i):
            copy.start()

    first[3].wait()
    for copy in lin_copies:
        copy.wait_recv()
    share = remote(lin.at[:, core], lin.at[:, core], sib.at[0], sib.at[1], sibling)
    share.start()
    share.wait_recv()

    inverse = lin[...].reshape(order, order)
    for copy in second:
        copy.wait()
    piece = 4
    for j in range(0, pcol_v.shape[0], piece):
        part = pcv[j : j + piece].reshape(piece * rank, order)
        pcl[j : j + piece] = nt(part, inverse).astype(HALF).reshape(piece, rank, order)
    prl[...] = nt(pvo[...].reshape(held * rank, order), inverse).astype(HALF).reshape(prl.shape)
    solved = [
        pltpu.make_async_copy(pcl, pcol_l, local.at[7]),
        pltpu.make_async_copy(prl, prow_l, local.at[8]),
    ]
    for copy in solved:
        copy.start()

    def g_remote(h, dy, dc_core, recv):
        return remote(
            gt.at[h], gt.at[h], gs.at[2 * dy + h], gr.at[recv], dev(x, y + dy, z, dc_core)
        )

    source = (y == x) & (core == z // 2)

    @pl.when(source)
    def _():
        base = cols * (z % 2)
        for h in range(2):
            j = base + 4 * h
            qu = pcu[pl.ds(j, 4)].reshape(4 * rank, order)
            cl = pcl[pl.ds(j, 4)].reshape(4 * rank, order)
            gt[h] = sketch_of(om[...], qu, cl, rank).astype(HALF)
            for dy in (1, 3, 2):
                g_remote(h, dy, h, 0).start()
            g_remote(h, 0, 1 - core, (core + h + 1) % 2).start()

    @pl.when(jnp.logical_not(source))
    def _():
        remote(gt.at[core], gt.at[core], gs.at[0], gr.at[0], sibling).wait_recv()

    @pl.when(y != x)
    def _():
        remote(gt.at[core], gt.at[core], gs.at[0], gr.at[1], sibling).start()

    @pl.when(jnp.logical_not(source))
    def _():
        remote(gt.at[1 - core], gt.at[1 - core], gs.at[0], gr.at[1], sibling).wait_recv()

    for e in range(2):
        for which in range(2):
            src, dst = ((prow_u, pu), (prow_v, pv))[which]
            into = dst.at[pl.ds(held * e, held)]

            @pl.when(jnp.logical_not(from_self[e]))
            def _():
                remote(src, into, prs.at[0], prr.at[2 * e + which], sibling).wait_recv()

    for i in range(2):
        for which in range(2):
            src, dst = ((prow_u, pu), (prow_v, pv))[which]

            @pl.when(to_self[i])
            def _():
                pltpu.make_async_copy(
                    src, dst.at[pl.ds(place, held)], prs.at[2 * i + which]
                ).wait()

    lanes = lax.broadcasted_iota(jnp.int32, (cols * rank, 2 * rank), 1)

    def pair(ii, carry):
        near_v = pv[pl.ds(2 * ii, 2)].reshape(2 * rank, order)
        near_u = pu[pl.ds(2 * ii, 2)].reshape(2 * rank, order)
        near_l = nt(near_v, lin[...].reshape(order, order)).astype(HALF)
        coupled = nt(gt[...].reshape(cols * rank, order), near_l).astype(HALF)
        for b in range(2):
            i = 2 * ii + b
            for copy in block_copies(i):
                copy.wait()
            mine = jnp.where(lanes // rank == b, coupled, jnp.zeros_like(coupled))
            for h in range(2):
                v = bv[i, 4 * h : 4 * h + 4].reshape(4 * rank, order)
                u = bu[i, 4 * h : 4 * h + 4].reshape(4 * rank, order)
                part = sketch_of(om[...], v, u, rank)
                part = part - nn(mine[4 * rank * h : 4 * rank * (h + 1)], near_u)
                bv[i, 4 * h : 4 * h + 4] = part.astype(HALF).reshape(4, rank, order)
            pltpu.make_async_copy(bv.at[i], t_out.at[i], tsem.at[i]).start()
        return carry

    lax.fori_loop(0, rows // 2, pair, 0)

    for i in range(rows):
        pltpu.make_async_copy(bv.at[i], t_out.at[i], tsem.at[i]).wait()
    for copy in solved:
        copy.wait()
    for copy in lin_copies:
        copy.wait_send()
    share.wait_send()

    @pl.when(source)
    def _():
        for h in range(2):
            for dy in (1, 3, 2):
                g_remote(h, dy, h, 0).wait_send()
            g_remote(h, 0, 1 - core, 0).wait_send()

    @pl.when(y != x)
    def _():
        remote(gt.at[core], gt.at[core], gs.at[0], gr.at[1], sibling).wait_send()

    for i in range(2):
        for which in range(2):
            @pl.when(jnp.logical_not(to_self[i]))
            def _():
                panel_copy(i, dev(targets[i], x, to_z, z // 2), which).wait_send()

    for copy in child_copies:
        copy.wait()


def finish_kernel(
    t_in, rcv, lab, prow_in, pcol_in, sketch, prow_l, pcol_l,
    tv, rv, head, following, tsem, osem, sems,
):
    rows, cols = t_in.shape[0], t_in.shape[1]
    slots = rcv.shape[0]
    loads = [pltpu.make_async_copy(rcv, rv, sems.at[0])]
    passed = [
        pltpu.make_async_copy(prow_in, prow_l, sems.at[1]),
        pltpu.make_async_copy(pcol_in, pcol_l, sems.at[2]),
    ]

    def load(i):
        return pltpu.make_async_copy(t_in.at[i], tv.at[i], tsem.at[i])

    def store(i):
        return pltpu.make_async_copy(tv.at[i], sketch.at[i], osem.at[i])

    load(0).start()
    loads[0].start()
    for i in range(1, rows):
        load(i).start()
    for copy in passed:
        copy.start()

    def clear(m, carry):
        head[m] = -1
        return carry

    lax.fori_loop(0, rows * cols, clear, 0, unroll=8)

    def link(s, carry):
        label = lab[s // 2, 0, s % 2]

        @pl.when(label >= 0)
        def _():
            following[s] = head[label]
            head[label] = s

        return carry

    lax.fori_loop(0, slots, link, 0)
    loads[0].wait()

    def one_row(i, carry):
        load(i).wait()

        def one_block(j, carry):
            slot = head[i * cols + j]

            @pl.when(slot >= 0)
            def _():
                def add(state):
                    s, total = state
                    return following[s], total + rv[s].astype(FULL)

                _, total = lax.while_loop(
                    lambda state: state[0] >= 0, add, (slot, tv[i, j].astype(FULL))
                )
                tv[i, j] = total.astype(HALF)

            return carry

        lax.fori_loop(0, cols, one_block, 0)
        store(i).start()
        return carry

    lax.fori_loop(0, rows, one_row, 0)
    for i in range(rows):
        store(i).wait()
    for copy in passed:
        copy.wait()


def body(
    blk_u, blk_v, prow_u, prow_v, pcol_u, pcol_v, linv, omega, child_u, child_v, child_dest,
    child_block,
):
    rows, cols, rank, order = blk_u.shape
    held, held_cols, count = prow_u.shape[0], pcol_u.shape[0], child_u.shape[0]
    anywhere = pl.BlockSpec(memory_space=pl.ANY)
    scalars = pl.BlockSpec(memory_space=pltpu.SMEM)
    dma = pltpu.SemaphoreType.DMA

    def half(*shape):
        return pltpu.VMEM(shape, HALF)

    partial, received, labels, row_solved, col_solved = pl.pallas_call(
        exchange_kernel,
        out_shape=(
            jax.ShapeDtypeStruct(blk_u.shape, HALF),
            jax.ShapeDtypeStruct((COLS, 2 * rank, order), HALF),
            jax.ShapeDtypeStruct((COLS, 8, 128), jnp.int32),
            jax.ShapeDtypeStruct(prow_v.shape, HALF),
            jax.ShapeDtypeStruct(pcol_v.shape, HALF),
        ),
        in_specs=[anywhere] * 10 + [scalars] * 2,
        out_specs=(anywhere,) * 5,
        scratch_shapes=[
            half(count, rank, order),
            half(count, rank, order),
            half(rank, order),
            half(COLS, 2 * rank, order),
            pltpu.VMEM((COLS, 8, 128), jnp.int32),
            half(COLS, 2, linv.shape[0] // 2, order),
            half(rows, rank, order),
            half(rows, rank, order),
            half(*blk_u.shape),
            half(*blk_v.shape),
            half(held_cols, rank, order),
            half(held_cols, rank, order),
            half(held_cols, rank, order),
            half(held, rank, order),
            half(held, rank, order),
            half(2, cols * rank // 2, order),
            dma((9,)),
            dma((COLS,)),
            dma((COLS,)),
            dma((COLS,)),
            dma((COLS,)),
            dma((COLS,)),
            dma((COLS,)),
            dma((2,)),
            dma((4,)),
            dma((4,)),
            dma((8,)),
            dma((2,)),
            dma((2, rows)),
            dma((rows,)),
        ],
        compiler_params=pltpu.CompilerParams(
            collective_id=0, has_side_effects=True, vmem_limit_bytes=52 * 2**20
        ),
        name="exchange",
    )(
        blk_u, blk_v, prow_u, prow_v, pcol_u, pcol_v, linv, omega, child_u, child_v, child_dest,
        child_block,
    )
    return pl.pallas_call(
        finish_kernel,
        out_shape=(
            jax.ShapeDtypeStruct(blk_u.shape, HALF),
            jax.ShapeDtypeStruct(prow_v.shape, HALF),
            jax.ShapeDtypeStruct(pcol_v.shape, HALF),
        ),
        in_specs=[anywhere, anywhere, scalars, anywhere, anywhere],
        out_specs=(anywhere,) * 3,
        scratch_shapes=[
            half(*blk_u.shape),
            half(2 * COLS, rank, order),
            pltpu.SMEM((rows * cols,), jnp.int32),
            pltpu.SMEM((2 * COLS,), jnp.int32),
            dma((rows,)),
            dma((rows,)),
            dma((3,)),
        ],
        compiler_params=pltpu.CompilerParams(vmem_limit_bytes=32 * 2**20),
        name="finish",
    )(partial, received.reshape(2 * COLS, rank, order), labels, row_solved, col_solved)


def solution(mesh):
    in_specs = (
        P("row", "col", None, None),
        P("row", "col", None, None),
        P("col", None, None),
        P("col", None, None),
        P("row", None, None),
        P("row", None, None),
        P("col", None),
        P(),
        P(("row", "col"), None, None),
        P(("row", "col"), None, None),
        P(("row", "col"), None),
        P(("row", "col")),
    )
    out_specs = (P("row", "col", None, None), P("col", None, None), P("row", None, None))
    return jax.shard_map(body, mesh=mesh, in_specs=in_specs, out_specs=out_specs, check_vma=False)
```

```python
import functools

import jax
import jax.numpy as jnp
from jax import lax
from jax.experimental import pallas as pl
from jax.experimental.pallas import tpu as pltpu
from jax.sharding import PartitionSpec as P

MESH = pl.DeviceIdType.MESH
HALF = jnp.bfloat16
FULL = jnp.float32
SIDE = 4
ROWS, COLS = 2 * SIDE, SIDE * SIDE
OFFSETS = sorted(
    [(dx, dz) for dx in range(SIDE) for dz in range(SIDE)],
    key=lambda o: (o == (0, 0), min(o[0], SIDE - o[0]) + min(o[1], SIDE - o[1])),
)


def nt(a, b):
    return lax.dot_general(a, b, (((1,), (1,)), ((), ())), preferred_element_type=FULL)


def nn(a, b):
    return lax.dot_general(a, b, (((1,), (0,)), ((), ())), preferred_element_type=FULL)


def block_diagonal(a, rank):
    n = a.shape[1] // rank
    tall = jnp.concatenate([a] * n, 0)
    row = lax.broadcasted_iota(jnp.int32, tall.shape, 0) // rank
    col = lax.broadcasted_iota(jnp.int32, tall.shape, 1) // rank
    return jnp.where(row == col, tall, jnp.zeros_like(tall))


def sketch_of(om, v, u, rank):
    proj = nt(om, v).astype(HALF)
    return nn(block_diagonal(proj, rank), u)


def exchange_kernel(
    blk_u, blk_v, prow_u, prow_v, pcol_u, pcol_v, linv, omega, child_u, child_v, child_dest, child_block,
    t_out, rcv, lab, prow_l, pcol_l,
    cu, cv, om, snd, lsnd, lin, pu, pv, bu, bv, pcu, pcv, pcl, pvo, prl, gt,
    vq, cdest, cblock, local, chs, chr_, las, lar, lis, lir, sib, us, ur, vs, vr, gs, gr, bsem, tsem,
):
    row, col = lax.axis_index("row"), lax.axis_index("col")
    x, z = col // SIDE, col % SIDE
    y, core = row // 2, row % 2
    rank, order = om.shape
    held = prow_v.shape[0]
    half_rows = linv.shape[0] // 2
    count = child_u.shape[0]
    rows, cols = blk_u.shape[0], blk_u.shape[1]

    def dev(x, y, z, core):
        return (2 * (y % SIDE) + core % 2, SIDE * (x % SIDE) + z % SIDE)

    sibling = dev(x, y, z, 1 - core)

    def remote(src, dst, send, recv, to):
        return pltpu.make_async_remote_copy(
            src_ref=src, dst_ref=dst, send_sem=send, recv_sem=recv, device_id=to,
            device_id_type=MESH,
        )

    first = [
        pltpu.make_async_copy(child_v, cv, local.at[0]),
        pltpu.make_async_copy(child_u, cu, local.at[1]),
        pltpu.make_async_copy(omega, om, local.at[2]),
        pltpu.make_async_copy(
            linv.at[pl.ds(half_rows * core, half_rows)], lin.at[col, core], local.at[3]
        ),
    ]
    scalar_copies = [
        pltpu.make_async_copy(child_dest, cdest, local.at[9]),
        pltpu.make_async_copy(child_block, cblock, local.at[10]),
    ]
    for copy in scalar_copies + first:
        copy.start()

    barrier = pltpu.get_barrier_semaphore()

    def greet(to):
        pl.semaphore_signal(barrier, 1, device_id=to, device_id_type=MESH)

    for dx, dz in OFFSETS[:-1]:
        greet(dev(x + dx, y, z + dz, core))
    greet(sibling)
    source = (y == x) & (core == z // 2)
    to_self = x == y
    awaited = COLS + 1 + jnp.where(source, 2 * (SIDE - 1), 0) - jnp.where(to_self, 3, 0)
    awaited += 2 * SIDE

    @pl.when(source)
    def _():
        for dy in range(1, SIDE):
            for dc in range(2):
                greet(dev(x, y + dy, z, dc))

    @pl.when(y != x)
    def _():
        greet(dev(x, x, z, z // 2))

    for i in range(SIDE):
        @pl.when(jnp.logical_not(to_self & (i == x)))
        def _():
            greet(dev(i, x, z, core))
            greet(dev(y, i, z, core))

    pl.semaphore_wait(barrier, awaited)

    lin_copies = []
    for o, (dx, dz) in enumerate(OFFSETS[:-1]):
        copy = remote(
            linv.at[pl.ds(half_rows * core, half_rows)], lin.at[col, core],
            lis.at[o], lir.at[o], dev(x + dx, y, z + dz, core),
        )
        copy.start()
        lin_copies.append(copy)

    place = pl.ds(held * (z % 2), held)
    fourth = rank // SIDE
    quarter = pl.ds(fourth * y, fourth)
    keeper = core == z // 2

    def u_first(i):
        return remote(
            prow_u.at[:, quarter], pu.at[place, quarter], us.at[i], ur.at[y], dev(i, x, z, core)
        )

    def u_second(dz):
        return remote(
            pu.at[place], pu.at[place], us.at[SIDE + dz], ur.at[SIDE + z % 2],
            dev(x, y, z + dz, core),
        )

    def v_first(dz):
        return remote(
            prow_v.at[:, quarter], vq.at[place], vs.at[SIDE + dz], vr.at[SIDE + z % 2],
            dev(x, y, z + dz, core),
        )

    def v_second(i):
        return remote(vq, pv.at[:, quarter], vs.at[i], vr.at[y], dev(i, x, z, core))

    def unless_self(i):
        return pl.when(jnp.logical_not(to_self & (i == x)))

    @pl.when(keeper)
    def _():
        for dz in (1, 3, 2):
            v_first(dz).start()
        pltpu.make_async_copy(prow_v.at[:, quarter], vq.at[place], vr.at[SIDE + z % 2]).start()
        for i in range(SIDE):
            @unless_self(i)
            def _():
                u_first(i).start()

        @pl.when(to_self)
        def _():
            pltpu.make_async_copy(
                prow_u.at[:, quarter], pu.at[place, quarter], ur.at[y]
            ).start()

    def pass_v():
        for e in range(2):
            mine = vq.at[pl.ds(held * e, held)]
            remote(mine, mine, vs.at[0], vr.at[SIDE + e], sibling).wait_recv()
        for i in range(SIDE):
            @unless_self(i)
            def _():
                v_second(i).start()

        @pl.when(to_self)
        def _():
            pltpu.make_async_copy(vq, pv.at[:, quarter], vr.at[y]).start()

    def pass_u():
        @pl.when(keeper)
        def _():
            for q in range(SIDE):
                mine = pu.at[place, pl.ds(fourth * q, fourth)]
                remote(mine, mine, us.at[0], ur.at[q], sibling).wait_recv()
            for dz in (1, 3, 2):
                u_second(dz).start()

    for copy in scalar_copies + first[:3]:
        copy.wait()
    lane = lax.broadcasted_iota(jnp.int32, lsnd.shape[1:], 1)
    child_copies = []
    for o, (dx, dz) in enumerate(OFFSETS):
        if o == 2:
            pass_v()
        if o == 4:
            pass_u()
        dest = SIDE * ((x + dx) % SIDE) + (z + dz) % SIDE

        def find(c, found, dest=dest):
            one, two = found
            hit = cdest[c] == dest
            two = jnp.where(hit & (one >= 0), c, two)
            one = jnp.where(hit & (one < 0), c, one)
            return one, two

        one, two = lax.fori_loop(0, count, find, (jnp.int32(-1), jnp.int32(-1)))
        label_one = jnp.where(one >= 0, cblock[jnp.maximum(one, 0)], -1)
        label_two = jnp.where(two >= 0, cblock[jnp.maximum(two, 0)], -1)
        one, two = jnp.maximum(one, 0), jnp.maximum(two, 0)
        lsnd[o] = jnp.where(lane == 0, label_one, label_two)
        v = jnp.concatenate([cv[one], cv[two]], 0)
        u = jnp.concatenate([cu[one], cu[two]], 0)
        snd[o] = sketch_of(om[...], v, u, rank).astype(HALF)
        if (dx, dz) == (0, 0):
            copies = [
                pltpu.make_async_copy(snd.at[o], rcv.at[col], chs.at[o]),
                pltpu.make_async_copy(lsnd.at[o], lab.at[col], las.at[o]),
            ]
        else:
            to = dev(x + dx, y, z + dz, core)
            copies = [
                remote(snd.at[o], rcv.at[col], chs.at[o], chr_.at[o], to),
                remote(lsnd.at[o], lab.at[col], las.at[o], lar.at[o], to),
            ]
        for copy in copies:
            copy.start()
        child_copies += copies

    second = [
        pltpu.make_async_copy(pcol_v, pcv, local.at[4]),
        pltpu.make_async_copy(prow_v, pvo, local.at[5]),
        pltpu.make_async_copy(pcol_u, pcu, local.at[6]),
    ]
    for copy in second:
        copy.start()

    def block_copies(i):
        return (
            pltpu.make_async_copy(blk_u.at[i], bu.at[i], bsem.at[0, i]),
            pltpu.make_async_copy(blk_v.at[i], bv.at[i], bsem.at[1, i]),
        )

    for i in range(rows):
        for copy in block_copies(i):
            copy.start()

    first[3].wait()
    for copy in lin_copies:
        copy.wait_recv()
    share = remote(lin.at[:, core], lin.at[:, core], sib.at[0], sib.at[1], sibling)
    share.start()
    share.wait_recv()

    inverse = lin[...].reshape(order, order)
    for copy in second:
        copy.wait()
    piece = 4
    for j in range(0, pcol_v.shape[0], piece):
        part = pcv[j : j + piece].reshape(piece * rank, order)
        pcl[j : j + piece] = nt(part, inverse).astype(HALF).reshape(piece, rank, order)
    prl[...] = nt(pvo[...].reshape(held * rank, order), inverse).astype(HALF).reshape(prl.shape)
    solved = [
        pltpu.make_async_copy(pcl, pcol_l, local.at[7]),
        pltpu.make_async_copy(prl, prow_l, local.at[8]),
    ]
    for copy in solved:
        copy.start()

    def g_remote(h, dy, dc_core, recv):
        return remote(
            gt.at[h], gt.at[h], gs.at[2 * dy + h], gr.at[recv], dev(x, y + dy, z, dc_core)
        )

    @pl.when(source)
    def _():
        base = cols * (z % 2)
        for h in range(2):
            j = base + 4 * h
            qu = pcu[pl.ds(j, 4)].reshape(4 * rank, order)
            cl = pcl[pl.ds(j, 4)].reshape(4 * rank, order)
            gt[h] = sketch_of(om[...], qu, cl, rank).astype(HALF)
            for dy in (1, 3, 2):
                g_remote(h, dy, h, 0).start()
            g_remote(h, 0, 1 - core, (core + h + 1) % 2).start()

    @pl.when(jnp.logical_not(source))
    def _():
        remote(gt.at[core], gt.at[core], gs.at[0], gr.at[0], sibling).wait_recv()

    @pl.when(y != x)
    def _():
        remote(gt.at[core], gt.at[core], gs.at[0], gr.at[1], sibling).start()

    @pl.when(jnp.logical_not(source))
    def _():
        remote(gt.at[1 - core], gt.at[1 - core], gs.at[0], gr.at[1], sibling).wait_recv()

    for e in range(2):
        mine = pu.at[pl.ds(held * e, held)]

        @pl.when(jnp.logical_not(keeper & (e == z % 2)))
        def _():
            remote(mine, mine, us.at[0], ur.at[SIDE + e], sibling).wait_recv()

    for q in range(SIDE):
        mine = pv.at[:, pl.ds(fourth * q, fourth)]
        remote(mine, mine, vs.at[0], vr.at[q], sibling).wait_recv()

    lanes = lax.broadcasted_iota(jnp.int32, (cols * rank, 2 * rank), 1)

    def pair(ii, carry):
        near_v = pv[pl.ds(2 * ii, 2)].reshape(2 * rank, order)
        near_u = pu[pl.ds(2 * ii, 2)].reshape(2 * rank, order)
        near_l = nt(near_v, lin[...].reshape(order, order)).astype(HALF)
        coupled = nt(gt[...].reshape(cols * rank, order), near_l).astype(HALF)
        for b in range(2):
            i = 2 * ii + b
            for copy in block_copies(i):
                copy.wait()
            mine = jnp.where(lanes // rank == b, coupled, jnp.zeros_like(coupled))
            for h in range(2):
                v = bv[i, 4 * h : 4 * h + 4].reshape(4 * rank, order)
                u = bu[i, 4 * h : 4 * h + 4].reshape(4 * rank, order)
                part = sketch_of(om[...], v, u, rank)
                part = part - nn(mine[4 * rank * h : 4 * rank * (h + 1)], near_u)
                bv[i, 4 * h : 4 * h + 4] = part.astype(HALF).reshape(4, rank, order)
            pltpu.make_async_copy(bv.at[i], t_out.at[i], tsem.at[i]).start()
        return carry

    lax.fori_loop(0, rows // 2, pair, 0)

    for i in range(rows):
        pltpu.make_async_copy(bv.at[i], t_out.at[i], tsem.at[i]).wait()
    for copy in solved:
        copy.wait()
    for copy in lin_copies:
        copy.wait_send()
    share.wait_send()

    @pl.when(source)
    def _():
        for h in range(2):
            for dy in (1, 3, 2):
                g_remote(h, dy, h, 0).wait_send()
            g_remote(h, 0, 1 - core, 0).wait_send()

    @pl.when(y != x)
    def _():
        remote(gt.at[core], gt.at[core], gs.at[0], gr.at[1], sibling).wait_send()

    @pl.when(keeper)
    def _():
        for dz in (1, 3, 2):
            v_first(dz).wait_send()
            u_second(dz).wait_send()
        for i in range(SIDE):
            @unless_self(i)
            def _():
                u_first(i).wait_send()

    for i in range(SIDE):
        @unless_self(i)
        def _():
            v_second(i).wait_send()

    for copy in child_copies:
        copy.wait()


def finish_kernel(
    partial, rcv, lab, prow_in, pcol_in, sketch, prow_l, pcol_l, fixed, head, following, osem, sems,
):
    rows, cols = partial.shape[0], partial.shape[1]
    slots = 2 * rcv.shape[0]
    rank = partial.shape[2]
    passed = [
        pltpu.make_async_copy(prow_in, prow_l, sems.at[0]),
        pltpu.make_async_copy(pcol_in, pcol_l, sems.at[1]),
    ]
    for copy in passed:
        copy.start()

    def clear(m, carry):
        head[m] = -1
        return carry

    lax.fori_loop(0, rows * cols, clear, 0, unroll=8)

    def link(s, carry):
        label = lab[s // 2, 0, s % 2]

        @pl.when(label >= 0)
        def _():
            following[s] = head[label]
            head[label] = s

        return carry

    lax.fori_loop(0, slots, link, 0)

    def one_row(i, carry):
        def one_block(j, carry):
            slot = head[i * cols + j]

            @pl.when(slot < 0)
            def _():
                pltpu.make_async_copy(partial.at[i, j], sketch.at[i, j], osem.at[i]).start()

            @pl.when(slot >= 0)
            def _():
                def add(state):
                    s, total = state
                    term = rcv[s // 2, pl.ds(pl.multiple_of(rank * (s % 2), rank), rank)]
                    return following[s], total + term.astype(FULL)

                _, total = lax.while_loop(
                    lambda state: state[0] >= 0, add, (slot, partial[i, j].astype(FULL))
                )
                fixed[i, j] = total.astype(HALF)
                pltpu.make_async_copy(fixed.at[i, j], sketch.at[i, j], osem.at[i]).start()

            return carry

        return lax.fori_loop(0, cols, one_block, carry)

    lax.fori_loop(0, rows, one_row, 0)
    for i in range(rows):
        pltpu.make_async_copy(fixed.at[i], sketch.at[i], osem.at[i]).wait()
    for copy in passed:
        copy.wait()


def body(
    blk_u, blk_v, prow_u, prow_v, pcol_u, pcol_v, linv, omega, child_u, child_v, child_dest,
    child_block,
):
    arguments = (
        blk_u, blk_v, prow_u, prow_v, pcol_u, pcol_v, linv, omega, child_u, child_v,
        child_dest[:, 0], child_block,
    )
    rows, cols, rank, order = blk_u.shape
    held, held_cols, count = prow_u.shape[0], pcol_u.shape[0], child_u.shape[0]
    anywhere = pl.BlockSpec(memory_space=pl.ANY)
    inside = pl.BlockSpec(memory_space=pltpu.VMEM)
    scalars = pl.BlockSpec(memory_space=pltpu.SMEM)
    dma = pltpu.SemaphoreType.DMA

    def half(*shape):
        return pltpu.VMEM(shape, HALF)

    partial, received, labels, row_solved, col_solved = pl.pallas_call(
        exchange_kernel,
        out_shape=(
            pltpu.VMEM(blk_u.shape, HALF),
            pltpu.VMEM((COLS, 2 * rank, order), HALF),
            pltpu.VMEM((COLS, 8, 128), jnp.int32),
            pltpu.VMEM(prow_v.shape, HALF),
            pltpu.VMEM(pcol_v.shape, HALF),
        ),
        in_specs=[anywhere] * 12,
        out_specs=(anywhere,) * 5,
        scratch_shapes=[
            half(count, rank, order),
            half(count, rank, order),
            half(rank, order),
            half(COLS, 2 * rank, order),
            pltpu.VMEM((COLS, 8, 128), jnp.int32),
            half(COLS, 2, linv.shape[0] // 2, order),
            half(rows, rank, order),
            half(rows, rank, order),
            half(*blk_u.shape),
            half(*blk_v.shape),
            half(held_cols, rank, order),
            half(held_cols, rank, order),
            half(held_cols, rank, order),
            half(held, rank, order),
            half(held, rank, order),
            half(2, cols * rank // 2, order),
            half(rows, rank // SIDE, order),
            pltpu.SMEM(child_block.shape, jnp.int32),
            pltpu.SMEM(child_block.shape, jnp.int32),
            dma((11,)),
            dma((COLS,)),
            dma((COLS,)),
            dma((COLS,)),
            dma((COLS,)),
            dma((COLS,)),
            dma((COLS,)),
            dma((2,)),
            dma((2 * SIDE,)),
            dma((SIDE + 2,)),
            dma((2 * SIDE,)),
            dma((SIDE + 2,)),
            dma((8,)),
            dma((2,)),
            dma((2, rows)),
            dma((rows,)),
        ],
        compiler_params=pltpu.CompilerParams(
            collective_id=0, has_side_effects=True, vmem_limit_bytes=48 * 2**20
        ),
        name="exchange",
    )(*(pltpu.with_memory_space_constraint(a, pltpu.HBM) for a in arguments))
    return pl.pallas_call(
        finish_kernel,
        out_shape=(
            jax.ShapeDtypeStruct(blk_u.shape, HALF),
            jax.ShapeDtypeStruct(prow_v.shape, HALF),
            jax.ShapeDtypeStruct(pcol_v.shape, HALF),
        ),
        in_specs=[inside, inside, scalars, anywhere, anywhere],
        out_specs=(anywhere,) * 3,
        scratch_shapes=[
            half(*blk_u.shape),
            pltpu.SMEM((rows * cols,), jnp.int32),
            pltpu.SMEM((2 * COLS,), jnp.int32),
            dma((rows,)),
            dma((2,)),
        ],
        compiler_params=pltpu.CompilerParams(vmem_limit_bytes=24 * 2**20),
        name="finish",
    )(
        pltpu.with_memory_space_constraint(partial, pltpu.VMEM),
        pltpu.with_memory_space_constraint(received, pltpu.VMEM),
        pltpu.with_memory_space_constraint(labels, pltpu.VMEM),
        pltpu.with_memory_space_constraint(row_solved, pltpu.VMEM),
        pltpu.with_memory_space_constraint(col_solved, pltpu.VMEM),
    )


def solution(mesh):
    in_specs = (
        P("row", "col", None, None),
        P("row", "col", None, None),
        P("col", None, None),
        P("col", None, None),
        P("row", None, None),
        P("row", None, None),
        P("col", None),
        P(),
        P(("row", "col"), None, None),
        P(("row", "col"), None, None),
        P(("row", "col"), None),
        P(("row", "col")),
    )
    out_specs = (P("row", "col", None, None), P("col", None, None), P("row", None, None))
    return jax.shard_map(body, mesh=mesh, in_specs=in_specs, out_specs=out_specs, check_vma=False)
```

```python
import functools

import jax
import jax.numpy as jnp
from jax import lax
from jax.experimental import pallas as pl
from jax.experimental.pallas import tpu as pltpu
from jax.sharding import PartitionSpec as P

MESH = pl.DeviceIdType.MESH
HALF = jnp.bfloat16
FULL = jnp.float32
SIDE = 4
ROWS, COLS = 2 * SIDE, SIDE * SIDE
OFFSETS = sorted(
    [(dx, dz) for dx in range(SIDE) for dz in range(SIDE)],
    key=lambda o: (o == (0, 0), min(o[0], SIDE - o[0]) + min(o[1], SIDE - o[1])),
)


def nt(a, b):
    return lax.dot_general(a, b, (((1,), (1,)), ((), ())), preferred_element_type=FULL)


def nn(a, b):
    return lax.dot_general(a, b, (((1,), (0,)), ((), ())), preferred_element_type=FULL)


def block_diagonal(a, rank):
    n = a.shape[1] // rank
    tall = jnp.concatenate([a] * n, 0)
    row = lax.broadcasted_iota(jnp.int32, tall.shape, 0) // rank
    col = lax.broadcasted_iota(jnp.int32, tall.shape, 1) // rank
    return jnp.where(row == col, tall, jnp.zeros_like(tall))


def sketch_of(om, v, u, rank):
    proj = nt(om, v).astype(HALF)
    return nn(block_diagonal(proj, rank), u)


def exchange_kernel(
    blk_u, blk_v, prow_u, prow_v, pcol_u, pcol_v, linv, omega, child_u, child_v, child_dest, child_block,
    t_out, rcv, lab, prow_l, pcol_l,
    cu, cv, om, snd, lsnd, lin, pu, pv, bu, bv, acc, pcu, pcv, pvo, et, gt,
    vq, cdest, cblock, local, chs, chr_, las, lar, lis, lir, sib, us, ur, vs, vr, gs, gr, bsem,
):
    row, col = lax.axis_index("row"), lax.axis_index("col")
    x, z = col // SIDE, col % SIDE
    y, core = row // 2, row % 2
    rank, order = om.shape
    held = prow_v.shape[0]
    half_rows = linv.shape[0] // 2
    count = child_u.shape[0]
    rows, cols = blk_u.shape[0], blk_u.shape[1]

    def dev(x, y, z, core):
        return (2 * (y % SIDE) + core % 2, SIDE * (x % SIDE) + z % SIDE)

    sibling = dev(x, y, z, 1 - core)

    def remote(src, dst, send, recv, to):
        return pltpu.make_async_remote_copy(
            src_ref=src, dst_ref=dst, send_sem=send, recv_sem=recv, device_id=to,
            device_id_type=MESH,
        )

    first = [
        pltpu.make_async_copy(child_v, cv, local.at[0]),
        pltpu.make_async_copy(child_u, cu, local.at[1]),
        pltpu.make_async_copy(omega, om, local.at[2]),
        pltpu.make_async_copy(
            linv.at[pl.ds(half_rows * core, half_rows)], lin.at[col, core], local.at[3]
        ),
    ]
    scalar_copies = [
        pltpu.make_async_copy(child_dest, cdest, local.at[9]),
        pltpu.make_async_copy(child_block, cblock, local.at[10]),
    ]
    second = [
        pltpu.make_async_copy(pcol_u, pcu, local.at[4]),
        pltpu.make_async_copy(pcol_v, pcv, local.at[5]),
        pltpu.make_async_copy(prow_v, pvo, local.at[6]),
    ]
    for copy in scalar_copies + first + second:
        copy.start()

    barrier = pltpu.get_barrier_semaphore()

    def greet(to):
        pl.semaphore_signal(barrier, 1, device_id=to, device_id_type=MESH)

    for dx, dz in OFFSETS[:-1]:
        greet(dev(x + dx, y, z + dz, core))
    greet(sibling)
    source = (y == x) & (core == z // 2)
    to_self = x == y
    awaited = COLS + 1 + jnp.where(source, 2 * (SIDE - 1), 0) - jnp.where(to_self, 3, 0)
    awaited += 2 * SIDE

    @pl.when(source)
    def _():
        for dy in range(1, SIDE):
            for dc in range(2):
                greet(dev(x, y + dy, z, dc))

    @pl.when(y != x)
    def _():
        greet(dev(x, x, z, z // 2))

    for i in range(SIDE):
        @pl.when(jnp.logical_not(to_self & (i == x)))
        def _():
            greet(dev(i, x, z, core))
            greet(dev(y, i, z, core))

    for copy in scalar_copies + first[:3]:
        copy.wait()
    lane = lax.broadcasted_iota(jnp.int32, lsnd.shape[1:], 1)

    def contribution(o):
        dx, dz = OFFSETS[o]
        dest = SIDE * ((x + dx) % SIDE) + (z + dz) % SIDE

        def find(c, found):
            one, two = found
            hit = cdest[c] == dest
            two = jnp.where(hit & (one >= 0), c, two)
            one = jnp.where(hit & (one < 0), c, one)
            return one, two

        one, two = lax.fori_loop(0, count, find, (jnp.int32(-1), jnp.int32(-1)), unroll=True)
        label_one = jnp.where(one >= 0, cblock[jnp.maximum(one, 0)], -1)
        label_two = jnp.where(two >= 0, cblock[jnp.maximum(two, 0)], -1)
        one, two = jnp.maximum(one, 0), jnp.maximum(two, 0)
        lsnd[o] = jnp.where(lane == 0, label_one, label_two)
        v = jnp.concatenate([cv[one], cv[two]], 0)
        u = jnp.concatenate([cu[one], cu[two]], 0)
        snd[o] = sketch_of(om[...], v, u, rank).astype(HALF)

    early = 2
    for o in range(early):
        contribution(o)

    for copy in second:
        copy.wait()

    @pl.when(source)
    def _():
        base = cols * (z % 2)
        for h in range(2):
            j = base + 4 * h
            qu = pcu[pl.ds(j, 4)].reshape(4 * rank, order)
            qv = pcv[pl.ds(j, 4)].reshape(4 * rank, order)
            et[h] = sketch_of(om[...], qu, qv, rank).astype(HALF)

    pl.semaphore_wait(barrier, awaited)

    def e_remote(h, dy, to_core, recv):
        return remote(
            et.at[h], et.at[h], gs.at[2 * dy + h], gr.at[recv], dev(x, y + dy, z, to_core)
        )

    @pl.when(source)
    def _():
        for h in range(2):
            for dy in (1, 3, 2):
                e_remote(h, dy, h, 0).start()
            e_remote(h, 0, 1 - core, (core + h + 1) % 2).start()

    place = pl.ds(held * (z % 2), held)
    fourth = rank // SIDE
    quarter = pl.ds(fourth * y, fourth)
    keeper = core == z // 2

    def u_first(i):
        return remote(
            prow_u.at[:, quarter], pu.at[place, quarter], us.at[i], ur.at[y], dev(i, x, z, core)
        )

    def u_second(dz):
        return remote(
            pu.at[place], pu.at[place], us.at[SIDE + dz], ur.at[SIDE + z % 2],
            dev(x, y, z + dz, core),
        )

    def v_first(dz):
        return remote(
            prow_v.at[:, quarter], vq.at[place], vs.at[SIDE + dz], vr.at[SIDE + z % 2],
            dev(x, y, z + dz, core),
        )

    def v_second(i):
        return remote(vq, pv.at[:, quarter], vs.at[i], vr.at[y], dev(i, x, z, core))

    def unless_self(i):
        return pl.when(jnp.logical_not(to_self & (i == x)))

    @pl.when(keeper)
    def _():
        for dz in (1, 3, 2):
            v_first(dz).start()
        pltpu.make_async_copy(prow_v.at[:, quarter], vq.at[place], vr.at[SIDE + z % 2]).start()
        for i in range(SIDE):
            @unless_self(i)
            def _():
                u_first(i).start()

        @pl.when(to_self)
        def _():
            pltpu.make_async_copy(
                prow_u.at[:, quarter], pu.at[place, quarter], ur.at[y]
            ).start()

    lin_copies = []
    for o, (dx, dz) in enumerate(OFFSETS[:-1]):
        copy = remote(
            linv.at[pl.ds(half_rows * core, half_rows)], lin.at[col, core],
            lis.at[o], lir.at[o], dev(x + dx, y, z + dz, core),
        )
        copy.start()
        lin_copies.append(copy)

    def pass_e():
        @pl.when(jnp.logical_not(source))
        def _():
            remote(et.at[core], et.at[core], gs.at[0], gr.at[0], sibling).wait_recv()

        @pl.when(y != x)
        def _():
            remote(et.at[core], et.at[core], gs.at[0], gr.at[1], sibling).start()

    def pass_v():
        for e in range(2):
            mine = vq.at[pl.ds(held * e, held)]
            remote(mine, mine, vs.at[0], vr.at[SIDE + e], sibling).wait_recv()
        for i in range(SIDE):
            @unless_self(i)
            def _():
                v_second(i).start()

        @pl.when(to_self)
        def _():
            pltpu.make_async_copy(vq, pv.at[:, quarter], vr.at[y]).start()

    def pass_u():
        @pl.when(keeper)
        def _():
            for q in range(SIDE):
                mine = pu.at[place, pl.ds(fourth * q, fourth)]
                remote(mine, mine, us.at[0], ur.at[q], sibling).wait_recv()
            for dz in (1, 3, 2):
                u_second(dz).start()

    child_copies = []
    for o, (dx, dz) in enumerate(OFFSETS):
        if o == 10:
            pass_v()
        if o == 2:
            pass_u()
        if o >= early:
            contribution(o)
        if (dx, dz) == (0, 0):
            copies = [
                pltpu.make_async_copy(snd.at[o], rcv.at[col], chs.at[o]),
                pltpu.make_async_copy(lsnd.at[o], lab.at[col], las.at[o]),
            ]
        else:
            to = dev(x + dx, y, z + dz, core)
            copies = [
                remote(snd.at[o], rcv.at[col], chs.at[o], chr_.at[o], to),
                remote(lsnd.at[o], lab.at[col], las.at[o], lar.at[o], to),
            ]
        for copy in copies:
            copy.start()
        child_copies += copies

    def block_copies(i):
        return (
            pltpu.make_async_copy(blk_u.at[i], bu.at[i], bsem.at[0, i]),
            pltpu.make_async_copy(blk_v.at[i], bv.at[i], bsem.at[1, i]),
        )

    for i in range(rows):
        for copy in block_copies(i):
            copy.start()

    pass_e()

    first[3].wait()
    for copy in lin_copies:
        copy.wait_recv()
    share = remote(lin.at[:, core], lin.at[:, core], sib.at[0], sib.at[1], sibling)
    share.start()

    def base_row(i, carry):
        for copy in block_copies(i):
            copy.wait()
        for h in range(2):
            v = bv[i, 4 * h : 4 * h + 4].reshape(4 * rank, order)
            u = bu[i, 4 * h : 4 * h + 4].reshape(4 * rank, order)
            acc[i, h] = sketch_of(om[...], v, u, rank)
        return carry

    lax.fori_loop(0, rows, base_row, 0)

    share.wait_recv()
    inverse = lin[...].reshape(order, order)
    piece = 4
    for j in range(0, pcol_v.shape[0], piece):
        part = pcv[j : j + piece].reshape(piece * rank, order)
        pcol_l[j : j + piece] = nt(part, inverse).astype(HALF).reshape(piece, rank, order)
    prow_l[...] = nt(pvo[...].reshape(held * rank, order), inverse).astype(HALF).reshape(
        prow_l.shape
    )

    @pl.when(jnp.logical_not(source))
    def _():
        remote(et.at[1 - core], et.at[1 - core], gs.at[0], gr.at[1], sibling).wait_recv()

    gt[...] = nt(et[...].reshape(gt.shape), inverse).astype(HALF)

    for e in range(2):
        mine = pu.at[pl.ds(held * e, held)]

        @pl.when(jnp.logical_not(keeper & (e == z % 2)))
        def _():
            remote(mine, mine, us.at[0], ur.at[SIDE + e], sibling).wait_recv()

    for q in range(SIDE):
        mine = pv.at[:, pl.ds(fourth * q, fourth)]
        remote(mine, mine, vs.at[0], vr.at[q], sibling).wait_recv()

    lanes = lax.broadcasted_iota(jnp.int32, (cols * rank, 2 * rank), 1)

    def pair(ii, carry):
        near_v = pv[pl.ds(2 * ii, 2)].reshape(2 * rank, order)
        near_u = pu[pl.ds(2 * ii, 2)].reshape(2 * rank, order)
        near_l = nt(near_v, lin[...].reshape(order, order)).astype(HALF)
        coupled = nt(gt[...], near_l).astype(HALF)
        for b in range(2):
            i = 2 * ii + b
            mine = jnp.where(lanes // rank == b, coupled, jnp.zeros_like(coupled))
            for h in range(2):
                update = nn(mine[4 * rank * h : 4 * rank * (h + 1)], near_u)
                t_out[i, 4 * h : 4 * h + 4] = (
                    (acc[i, h] - update).astype(HALF).reshape(4, rank, order)
                )
        return carry

    lax.fori_loop(0, rows // 2, pair, 0)

    for copy in lin_copies:
        copy.wait_send()
    share.wait_send()

    @pl.when(source)
    def _():
        for h in range(2):
            for dy in (1, 3, 2):
                e_remote(h, dy, h, 0).wait_send()
            e_remote(h, 0, 1 - core, 0).wait_send()

    @pl.when(y != x)
    def _():
        remote(et.at[core], et.at[core], gs.at[0], gr.at[1], sibling).wait_send()

    @pl.when(keeper)
    def _():
        for dz in (1, 3, 2):
            v_first(dz).wait_send()
            u_second(dz).wait_send()
        for i in range(SIDE):
            @unless_self(i)
            def _():
                u_first(i).wait_send()

    for i in range(SIDE):
        @unless_self(i)
        def _():
            v_second(i).wait_send()

    for copy in child_copies:
        copy.wait()


def finish_kernel(
    partial, rcv, lab, prow_in, pcol_in, sketch, prow_l, pcol_l, fixed, head, following, osem, sems,
):
    rows, cols = partial.shape[0], partial.shape[1]
    slots = 2 * rcv.shape[0]
    rank = partial.shape[2]
    passed = [
        pltpu.make_async_copy(prow_in, prow_l, sems.at[0]),
        pltpu.make_async_copy(pcol_in, pcol_l, sems.at[1]),
    ]
    for copy in passed:
        copy.start()

    def clear(m, carry):
        head[m] = -1
        return carry

    lax.fori_loop(0, rows * cols, clear, 0, unroll=8)

    def link(s, carry):
        label = lab[s // 2, 0, s % 2]

        @pl.when(label >= 0)
        def _():
            following[s] = head[label]
            head[label] = s

        return carry

    lax.fori_loop(0, slots, link, 0)

    def one_row(i, carry):
        def one_block(j, carry):
            slot = head[i * cols + j]

            @pl.when(slot < 0)
            def _():
                pltpu.make_async_copy(partial.at[i, j], sketch.at[i, j], osem.at[i]).start()

            @pl.when(slot >= 0)
            def _():
                def add(state):
                    s, total = state
                    term = rcv[s // 2, pl.ds(pl.multiple_of(rank * (s % 2), rank), rank)]
                    return following[s], total + term.astype(FULL)

                _, total = lax.while_loop(
                    lambda state: state[0] >= 0, add, (slot, partial[i, j].astype(FULL))
                )
                fixed[i, j] = total.astype(HALF)
                pltpu.make_async_copy(fixed.at[i, j], sketch.at[i, j], osem.at[i]).start()

            return carry

        return lax.fori_loop(0, cols, one_block, carry)

    lax.fori_loop(0, rows, one_row, 0)
    for i in range(rows):
        pltpu.make_async_copy(fixed.at[i], sketch.at[i], osem.at[i]).wait()
    for copy in passed:
        copy.wait()


def body(
    blk_u, blk_v, prow_u, prow_v, pcol_u, pcol_v, linv, omega, child_u, child_v, child_dest,
    child_block,
):
    arguments = (
        blk_u, blk_v, prow_u, prow_v, pcol_u, pcol_v, linv, omega, child_u, child_v,
        child_dest[:, 0], child_block,
    )
    rows, cols, rank, order = blk_u.shape
    held, held_cols, count = prow_u.shape[0], pcol_u.shape[0], child_u.shape[0]
    anywhere = pl.BlockSpec(memory_space=pl.ANY)
    inside = pl.BlockSpec(memory_space=pltpu.VMEM)
    scalars = pl.BlockSpec(memory_space=pltpu.SMEM)
    dma = pltpu.SemaphoreType.DMA

    def half(*shape):
        return pltpu.VMEM(shape, HALF)

    partial, received, labels, row_solved, col_solved = pl.pallas_call(
        exchange_kernel,
        out_shape=(
            pltpu.VMEM(blk_u.shape, HALF),
            pltpu.VMEM((COLS, 2 * rank, order), HALF),
            pltpu.VMEM((COLS, 1, 128), jnp.int32),
            pltpu.VMEM(prow_v.shape, HALF),
            pltpu.VMEM(pcol_v.shape, HALF),
        ),
        in_specs=[anywhere] * 12,
        out_specs=(inside, anywhere, anywhere, inside, inside),
        scratch_shapes=[
            half(count, rank, order),
            half(count, rank, order),
            half(rank, order),
            half(COLS, 2 * rank, order),
            pltpu.VMEM((COLS, 1, 128), jnp.int32),
            half(COLS, 2, linv.shape[0] // 2, order),
            half(rows, rank, order),
            half(rows, rank, order),
            half(*blk_u.shape),
            half(*blk_v.shape),
            pltpu.VMEM((rows, 2, cols * rank // 2, order), FULL),
            half(held_cols, rank, order),
            half(held_cols, rank, order),
            half(held, rank, order),
            half(2, cols * rank // 2, order),
            half(cols * rank, order),
            half(rows, rank // SIDE, order),
            pltpu.SMEM(child_block.shape, jnp.int32),
            pltpu.SMEM(child_block.shape, jnp.int32),
            dma((11,)),
            dma((COLS,)),
            dma((COLS,)),
            dma((COLS,)),
            dma((COLS,)),
            dma((COLS,)),
            dma((COLS,)),
            dma((2,)),
            dma((2 * SIDE,)),
            dma((SIDE + 2,)),
            dma((2 * SIDE,)),
            dma((SIDE + 2,)),
            dma((8,)),
            dma((2,)),
            dma((2, rows)),
        ],
        compiler_params=pltpu.CompilerParams(
            collective_id=0, has_side_effects=True, vmem_limit_bytes=48 * 2**20
        ),
        name="exchange",
    )(*(pltpu.with_memory_space_constraint(a, pltpu.HBM) for a in arguments))
    return pl.pallas_call(
        finish_kernel,
        out_shape=(
            jax.ShapeDtypeStruct(blk_u.shape, HALF),
            jax.ShapeDtypeStruct(prow_v.shape, HALF),
            jax.ShapeDtypeStruct(pcol_v.shape, HALF),
        ),
        in_specs=[inside, inside, scalars, anywhere, anywhere],
        out_specs=(anywhere,) * 3,
        scratch_shapes=[
            half(*blk_u.shape),
            pltpu.SMEM((rows * cols,), jnp.int32),
            pltpu.SMEM((2 * COLS,), jnp.int32),
            dma((rows,)),
            dma((2,)),
        ],
        compiler_params=pltpu.CompilerParams(vmem_limit_bytes=24 * 2**20),
        name="finish",
    )(
        pltpu.with_memory_space_constraint(partial, pltpu.VMEM),
        pltpu.with_memory_space_constraint(received, pltpu.VMEM),
        pltpu.with_memory_space_constraint(labels, pltpu.VMEM),
        pltpu.with_memory_space_constraint(row_solved, pltpu.VMEM),
        pltpu.with_memory_space_constraint(col_solved, pltpu.VMEM),
    )


def solution(mesh):
    in_specs = (
        P("row", "col", None, None),
        P("row", "col", None, None),
        P("col", None, None),
        P("col", None, None),
        P("row", None, None),
        P("row", None, None),
        P("col", None),
        P(),
        P(("row", "col"), None, None),
        P(("row", "col"), None, None),
        P(("row", "col"), None),
        P(("row", "col")),
    )
    out_specs = (P("row", "col", None, None), P("col", None, None), P("row", None, None))
    return jax.shard_map(body, mesh=mesh, in_specs=in_specs, out_specs=out_specs, check_vma=False)
```

```python
import functools

import jax
import jax.numpy as jnp
from jax import lax
from jax.experimental import pallas as pl
from jax.experimental.pallas import tpu as pltpu
from jax.sharding import PartitionSpec as P

MESH = pl.DeviceIdType.MESH
HALF = jnp.bfloat16
FULL = jnp.float32
SIDE = 4
ROWS, COLS = 2 * SIDE, SIDE * SIDE
OFFSETS = sorted(
    [(dx, dz) for dx in range(SIDE) for dz in range(SIDE)],
    key=lambda o: (o == (0, 0), min(o[0], SIDE - o[0]) + min(o[1], SIDE - o[1])),
)


def nt(a, b):
    return lax.dot_general(a, b, (((1,), (1,)), ((), ())), preferred_element_type=FULL)


def nn(a, b):
    return lax.dot_general(a, b, (((1,), (0,)), ((), ())), preferred_element_type=FULL)


def block_diagonal(a, rank):
    n = a.shape[1] // rank
    tall = jnp.concatenate([a] * n, 0)
    row = lax.broadcasted_iota(jnp.int32, tall.shape, 0) // rank
    col = lax.broadcasted_iota(jnp.int32, tall.shape, 1) // rank
    return jnp.where(row == col, tall, jnp.zeros_like(tall))


def sketch_of(om, v, u, rank):
    proj = nt(om, v).astype(HALF)
    return nn(block_diagonal(proj, rank), u)


def exchange_kernel(
    blk_u, blk_v, prow_u, prow_v, pcol_u, pcol_v, linv, omega, child_u, child_v, child_dest, child_block,
    t_out, rcv, lab, prow_l, pcol_l,
    cu, cv, om, snd, lsnd, lin, pu, pv, bu, bv, acc, pcu, pcv, pvo, et, gt,
    vq, cdest, cblock, local, chs, chr_, las, lar, lis, lir, sib, us, ur, vs, vr, gs, gr, bsem,
):
    row, col = lax.axis_index("row"), lax.axis_index("col")
    x, z = col // SIDE, col % SIDE
    y, core = row // 2, row % 2
    rank, order = om.shape
    held = prow_v.shape[0]
    half_rows = linv.shape[0] // 2
    count = child_u.shape[0]
    rows, cols = blk_u.shape[0], blk_u.shape[1]

    def dev(x, y, z, core):
        return (2 * (y % SIDE) + core % 2, SIDE * (x % SIDE) + z % SIDE)

    sibling = dev(x, y, z, 1 - core)

    def remote(src, dst, send, recv, to):
        return pltpu.make_async_remote_copy(
            src_ref=src, dst_ref=dst, send_sem=send, recv_sem=recv, device_id=to,
            device_id_type=MESH,
        )

    lin[...] = jnp.zeros_like(lin)

    first = [
        pltpu.make_async_copy(child_v, cv, local.at[0]),
        pltpu.make_async_copy(child_u, cu, local.at[1]),
        pltpu.make_async_copy(omega, om, local.at[2]),
        pltpu.make_async_copy(
            linv.at[pl.ds(half_rows * core, half_rows)], lin.at[col, core], local.at[3]
        ),
    ]
    scalar_copies = [
        pltpu.make_async_copy(child_dest, cdest, local.at[9]),
        pltpu.make_async_copy(child_block, cblock, local.at[10]),
    ]
    second = [
        pltpu.make_async_copy(pcol_u, pcu, local.at[4]),
        pltpu.make_async_copy(pcol_v, pcv, local.at[5]),
        pltpu.make_async_copy(prow_v, pvo, local.at[6]),
    ]
    for copy in scalar_copies + first + second:
        copy.start()

    barrier = pltpu.get_barrier_semaphore()

    def greet(to):
        pl.semaphore_signal(barrier, 1, device_id=to, device_id_type=MESH)

    for dx, dz in OFFSETS[:-1]:
        greet(dev(x + dx, y, z + dz, core))
    greet(sibling)
    source = (y == x) & (core == z // 2)
    to_self = x == y
    awaited = COLS + 1 + jnp.where(source, 2 * (SIDE - 1), 0) - jnp.where(to_self, 3, 0)
    awaited += 2 * SIDE

    @pl.when(source)
    def _():
        for dy in range(1, SIDE):
            for dc in range(2):
                greet(dev(x, y + dy, z, dc))

    @pl.when(y != x)
    def _():
        greet(dev(x, x, z, z // 2))

    for i in range(SIDE):
        @pl.when(jnp.logical_not(to_self & (i == x)))
        def _():
            greet(dev(i, x, z, core))
            greet(dev(y, i, z, core))

    for copy in scalar_copies + first[:3]:
        copy.wait()
    lane = lax.broadcasted_iota(jnp.int32, lsnd.shape[1:], 1)

    def contribution(o):
        dx, dz = OFFSETS[o]
        dest = SIDE * ((x + dx) % SIDE) + (z + dz) % SIDE

        def find(c, found):
            one, two = found
            hit = cdest[c] == dest
            two = jnp.where(hit & (one >= 0), c, two)
            one = jnp.where(hit & (one < 0), c, one)
            return one, two

        one, two = lax.fori_loop(0, count, find, (jnp.int32(-1), jnp.int32(-1)), unroll=True)
        label_one = jnp.where(one >= 0, cblock[jnp.maximum(one, 0)], -1)
        label_two = jnp.where(two >= 0, cblock[jnp.maximum(two, 0)], -1)
        one, two = jnp.maximum(one, 0), jnp.maximum(two, 0)
        lsnd[o] = jnp.where(lane == 0, label_one, label_two)
        v = jnp.concatenate([cv[one], cv[two]], 0)
        u = jnp.concatenate([cu[one], cu[two]], 0)
        snd[o] = sketch_of(om[...], v, u, rank).astype(HALF)

    early = 2
    for o in range(early):
        contribution(o)

    for copy in second:
        copy.wait()

    @pl.when(source)
    def _():
        base = cols * (z % 2)
        for h in range(2):
            j = base + 4 * h
            qu = pcu[pl.ds(j, 4)].reshape(4 * rank, order)
            qv = pcv[pl.ds(j, 4)].reshape(4 * rank, order)
            et[h] = sketch_of(om[...], qu, qv, rank).astype(HALF)

    pl.semaphore_wait(barrier, awaited)

    def e_remote(h, dy, to_core, recv):
        return remote(
            et.at[h], et.at[h], gs.at[2 * dy + h], gr.at[recv], dev(x, y + dy, z, to_core)
        )

    @pl.when(source)
    def _():
        for h in range(2):
            for dy in (1, 3, 2):
                e_remote(h, dy, h, 0).start()
            e_remote(h, 0, 1 - core, (core + h + 1) % 2).start()

    place = pl.ds(held * (z % 2), held)
    fourth = rank // SIDE
    quarter = pl.ds(fourth * y, fourth)
    keeper = core == z // 2

    def u_first(i):
        return remote(
            prow_u.at[:, quarter], pu.at[place, quarter], us.at[i], ur.at[y], dev(i, x, z, core)
        )

    def u_second(dz):
        return remote(
            pu.at[place], pu.at[place], us.at[SIDE + dz], ur.at[SIDE + z % 2],
            dev(x, y, z + dz, core),
        )

    def v_first(dz):
        return remote(
            prow_v.at[:, quarter], vq.at[place], vs.at[SIDE + dz], vr.at[SIDE + z % 2],
            dev(x, y, z + dz, core),
        )

    def v_second(i):
        return remote(vq, pv.at[:, quarter], vs.at[i], vr.at[y], dev(i, x, z, core))

    def unless_self(i):
        return pl.when(jnp.logical_not(to_self & (i == x)))

    @pl.when(keeper)
    def _():
        for dz in (1, 3, 2):
            v_first(dz).start()
        pltpu.make_async_copy(prow_v.at[:, quarter], vq.at[place], vr.at[SIDE + z % 2]).start()
        for i in range(SIDE):
            @unless_self(i)
            def _():
                u_first(i).start()

        @pl.when(to_self)
        def _():
            pltpu.make_async_copy(
                prow_u.at[:, quarter], pu.at[place, quarter], ur.at[y]
            ).start()

    def lin_copy(o, n):
        dx, dz = OFFSETS[o]
        tiles = pl.ds(0, order // SIDE * (n + 1))
        return remote(
            linv.at[pl.ds(half_rows * core, half_rows), tiles], lin.at[col, core, :, tiles],
            lis.at[o], lir.at[o], dev(x + dx, y, z + dz, core),
        )

    for n in range(SIDE):
        @pl.when(x == n)
        def _():
            for o in range(COLS - 1):
                lin_copy(o, n).start()

    def pass_e():
        @pl.when(jnp.logical_not(source))
        def _():
            remote(et.at[core], et.at[core], gs.at[0], gr.at[0], sibling).wait_recv()

        @pl.when(y != x)
        def _():
            remote(et.at[core], et.at[core], gs.at[0], gr.at[1], sibling).start()

    def pass_v():
        for e in range(2):
            mine = vq.at[pl.ds(held * e, held)]
            remote(mine, mine, vs.at[0], vr.at[SIDE + e], sibling).wait_recv()
        for i in range(SIDE):
            @unless_self(i)
            def _():
                v_second(i).start()

        @pl.when(to_self)
        def _():
            pltpu.make_async_copy(vq, pv.at[:, quarter], vr.at[y]).start()

    def pass_u():
        @pl.when(keeper)
        def _():
            for q in range(SIDE):
                mine = pu.at[place, pl.ds(fourth * q, fourth)]
                remote(mine, mine, us.at[0], ur.at[q], sibling).wait_recv()
            for dz in (1, 3, 2):
                u_second(dz).start()

    child_copies = []
    for o, (dx, dz) in enumerate(OFFSETS):
        if o == 10:
            pass_v()
        if o == 2:
            pass_u()
        if o >= early:
            contribution(o)
        if (dx, dz) == (0, 0):
            copies = [
                pltpu.make_async_copy(snd.at[o], rcv.at[col], chs.at[o]),
                pltpu.make_async_copy(lsnd.at[o], lab.at[col], las.at[o]),
            ]
        else:
            to = dev(x + dx, y, z + dz, core)
            copies = [
                remote(snd.at[o], rcv.at[col], chs.at[o], chr_.at[o], to),
                remote(lsnd.at[o], lab.at[col], las.at[o], lar.at[o], to),
            ]
        for copy in copies:
            copy.start()
        child_copies += copies

    def block_copies(i):
        return (
            pltpu.make_async_copy(blk_u.at[i], bu.at[i], bsem.at[0, i]),
            pltpu.make_async_copy(blk_v.at[i], bv.at[i], bsem.at[1, i]),
        )

    for i in range(rows):
        for copy in block_copies(i):
            copy.start()

    pass_e()

    first[3].wait()
    for n in range(SIDE):
        for turn in range(SIDE):
            @pl.when((x + SIDE - turn) % SIDE == n)
            def _():
                for o in range(COLS - 1):
                    if OFFSETS[o][0] == turn:
                        lin_copy(o, n).wait_recv()

    share = remote(lin.at[:, core], lin.at[:, core], sib.at[0], sib.at[1], sibling)
    share.start()

    def base_row(i, carry):
        for copy in block_copies(i):
            copy.wait()
        for h in range(2):
            v = bv[i, 4 * h : 4 * h + 4].reshape(4 * rank, order)
            u = bu[i, 4 * h : 4 * h + 4].reshape(4 * rank, order)
            acc[i, h] = sketch_of(om[...], v, u, rank)
        return carry

    lax.fori_loop(0, rows, base_row, 0)

    share.wait_recv()
    inverse = lin[...].reshape(order, order)
    piece = 4
    for j in range(0, pcol_v.shape[0], piece):
        part = pcv[j : j + piece].reshape(piece * rank, order)
        pcol_l[j : j + piece] = nt(part, inverse).astype(HALF).reshape(piece, rank, order)
    prow_l[...] = nt(pvo[...].reshape(held * rank, order), inverse).astype(HALF).reshape(
        prow_l.shape
    )

    @pl.when(jnp.logical_not(source))
    def _():
        remote(et.at[1 - core], et.at[1 - core], gs.at[0], gr.at[1], sibling).wait_recv()

    gt[...] = nt(et[...].reshape(gt.shape), inverse).astype(HALF)

    for e in range(2):
        mine = pu.at[pl.ds(held * e, held)]

        @pl.when(jnp.logical_not(keeper & (e == z % 2)))
        def _():
            remote(mine, mine, us.at[0], ur.at[SIDE + e], sibling).wait_recv()

    for q in range(SIDE):
        mine = pv.at[:, pl.ds(fourth * q, fourth)]
        remote(mine, mine, vs.at[0], vr.at[q], sibling).wait_recv()

    lanes = lax.broadcasted_iota(jnp.int32, (cols * rank, 2 * rank), 1)

    def pair(ii, carry):
        near_v = pv[pl.ds(2 * ii, 2)].reshape(2 * rank, order)
        near_u = pu[pl.ds(2 * ii, 2)].reshape(2 * rank, order)
        near_l = nt(near_v, lin[...].reshape(order, order)).astype(HALF)
        coupled = nt(gt[...], near_l).astype(HALF)
        for b in range(2):
            i = 2 * ii + b
            mine = jnp.where(lanes // rank == b, coupled, jnp.zeros_like(coupled))
            for h in range(2):
                update = nn(mine[4 * rank * h : 4 * rank * (h + 1)], near_u)
                t_out[i, 4 * h : 4 * h + 4] = (
                    (acc[i, h] - update).astype(HALF).reshape(4, rank, order)
                )
        return carry

    lax.fori_loop(0, rows // 2, pair, 0)

    for n in range(SIDE):
        @pl.when(x == n)
        def _():
            for o in range(COLS - 1):
                lin_copy(o, n).wait_send()

    share.wait_send()

    @pl.when(source)
    def _():
        for h in range(2):
            for dy in (1, 3, 2):
                e_remote(h, dy, h, 0).wait_send()
            e_remote(h, 0, 1 - core, 0).wait_send()

    @pl.when(y != x)
    def _():
        remote(et.at[core], et.at[core], gs.at[0], gr.at[1], sibling).wait_send()

    @pl.when(keeper)
    def _():
        for dz in (1, 3, 2):
            v_first(dz).wait_send()
            u_second(dz).wait_send()
        for i in range(SIDE):
            @unless_self(i)
            def _():
                u_first(i).wait_send()

    for i in range(SIDE):
        @unless_self(i)
        def _():
            v_second(i).wait_send()

    for copy in child_copies:
        copy.wait()


def finish_kernel(
    partial, rcv, lab, prow_in, pcol_in, sketch, prow_l, pcol_l, fixed, head, following, osem, sems,
):
    rows, cols = partial.shape[0], partial.shape[1]
    slots = 2 * rcv.shape[0]
    rank = partial.shape[2]
    passed = [
        pltpu.make_async_copy(prow_in, prow_l, sems.at[0]),
        pltpu.make_async_copy(pcol_in, pcol_l, sems.at[1]),
    ]
    for copy in passed:
        copy.start()

    def clear(m, carry):
        head[m] = -1
        return carry

    lax.fori_loop(0, rows * cols, clear, 0, unroll=8)

    def link(s, carry):
        label = lab[s // 2, 0, s % 2]

        @pl.when(label >= 0)
        def _():
            following[s] = head[label]
            head[label] = s

        return carry

    lax.fori_loop(0, slots, link, 0)

    def one_row(i, carry):
        def one_block(j, carry):
            slot = head[i * cols + j]

            @pl.when(slot < 0)
            def _():
                pltpu.make_async_copy(partial.at[i, j], sketch.at[i, j], osem.at[i]).start()

            @pl.when(slot >= 0)
            def _():
                def add(state):
                    s, total = state
                    term = rcv[s // 2, pl.ds(pl.multiple_of(rank * (s % 2), rank), rank)]
                    return following[s], total + term.astype(FULL)

                _, total = lax.while_loop(
                    lambda state: state[0] >= 0, add, (slot, partial[i, j].astype(FULL))
                )
                fixed[i, j] = total.astype(HALF)
                pltpu.make_async_copy(fixed.at[i, j], sketch.at[i, j], osem.at[i]).start()

            return carry

        return lax.fori_loop(0, cols, one_block, carry)

    lax.fori_loop(0, rows, one_row, 0)
    for i in range(rows):
        pltpu.make_async_copy(fixed.at[i], sketch.at[i], osem.at[i]).wait()
    for copy in passed:
        copy.wait()


def body(
    blk_u, blk_v, prow_u, prow_v, pcol_u, pcol_v, linv, omega, child_u, child_v, child_dest,
    child_block,
):
    arguments = (
        blk_u, blk_v, prow_u, prow_v, pcol_u, pcol_v, linv, omega, child_u, child_v,
        child_dest[:, 0], child_block,
    )
    rows, cols, rank, order = blk_u.shape
    held, held_cols, count = prow_u.shape[0], pcol_u.shape[0], child_u.shape[0]
    anywhere = pl.BlockSpec(memory_space=pl.ANY)
    inside = pl.BlockSpec(memory_space=pltpu.VMEM)
    scalars = pl.BlockSpec(memory_space=pltpu.SMEM)
    dma = pltpu.SemaphoreType.DMA

    def half(*shape):
        return pltpu.VMEM(shape, HALF)

    partial, received, labels, row_solved, col_solved = pl.pallas_call(
        exchange_kernel,
        out_shape=(
            pltpu.VMEM(blk_u.shape, HALF),
            pltpu.VMEM((COLS, 2 * rank, order), HALF),
            pltpu.VMEM((COLS, 1, 128), jnp.int32),
            pltpu.VMEM(prow_v.shape, HALF),
            pltpu.VMEM(pcol_v.shape, HALF),
        ),
        in_specs=[anywhere] * 12,
        out_specs=(inside, anywhere, anywhere, inside, inside),
        scratch_shapes=[
            half(count, rank, order),
            half(count, rank, order),
            half(rank, order),
            half(COLS, 2 * rank, order),
            pltpu.VMEM((COLS, 1, 128), jnp.int32),
            half(COLS, 2, linv.shape[0] // 2, order),
            half(rows, rank, order),
            half(rows, rank, order),
            half(*blk_u.shape),
            half(*blk_v.shape),
            pltpu.VMEM((rows, 2, cols * rank // 2, order), FULL),
            half(held_cols, rank, order),
            half(held_cols, rank, order),
            half(held, rank, order),
            half(2, cols * rank // 2, order),
            half(cols * rank, order),
            half(rows, rank // SIDE, order),
            pltpu.SMEM(child_block.shape, jnp.int32),
            pltpu.SMEM(child_block.shape, jnp.int32),
            dma((11,)),
            dma((COLS,)),
            dma((COLS,)),
            dma((COLS,)),
            dma((COLS,)),
            dma((COLS,)),
            dma((COLS,)),
            dma((2,)),
            dma((2 * SIDE,)),
            dma((SIDE + 2,)),
            dma((2 * SIDE,)),
            dma((SIDE + 2,)),
            dma((8,)),
            dma((2,)),
            dma((2, rows)),
        ],
        compiler_params=pltpu.CompilerParams(
            collective_id=0, has_side_effects=True, vmem_limit_bytes=48 * 2**20
        ),
        name="exchange",
    )(*(pltpu.with_memory_space_constraint(a, pltpu.HBM) for a in arguments))
    return pl.pallas_call(
        finish_kernel,
        out_shape=(
            jax.ShapeDtypeStruct(blk_u.shape, HALF),
            jax.ShapeDtypeStruct(prow_v.shape, HALF),
            jax.ShapeDtypeStruct(pcol_v.shape, HALF),
        ),
        in_specs=[inside, inside, scalars, anywhere, anywhere],
        out_specs=(anywhere,) * 3,
        scratch_shapes=[
            half(*blk_u.shape),
            pltpu.SMEM((rows * cols,), jnp.int32),
            pltpu.SMEM((2 * COLS,), jnp.int32),
            dma((rows,)),
            dma((2,)),
        ],
        compiler_params=pltpu.CompilerParams(vmem_limit_bytes=24 * 2**20),
        name="finish",
    )(
        pltpu.with_memory_space_constraint(partial, pltpu.VMEM),
        pltpu.with_memory_space_constraint(received, pltpu.VMEM),
        pltpu.with_memory_space_constraint(labels, pltpu.VMEM),
        pltpu.with_memory_space_constraint(row_solved, pltpu.VMEM),
        pltpu.with_memory_space_constraint(col_solved, pltpu.VMEM),
    )


def solution(mesh):
    in_specs = (
        P("row", "col", None, None),
        P("row", "col", None, None),
        P("col", None, None),
        P("col", None, None),
        P("row", None, None),
        P("row", None, None),
        P("col", None),
        P(),
        P(("row", "col"), None, None),
        P(("row", "col"), None, None),
        P(("row", "col"), None),
        P(("row", "col")),
    )
    out_specs = (P("row", "col", None, None), P("col", None, None), P("row", None, None))
    return jax.shard_map(body, mesh=mesh, in_specs=in_specs, out_specs=out_specs, check_vma=False)
```
